32 devices in a mesh: pair: 8 (over z, x), blk: 4 (over y, core).
Axes of the slice: x: 2, y: 2, z: 4, core: 2. Of those that a mesh axis runs over, the one named last changes fastest.
Arguments:
- integrals: bfloat16 [32, 4, 2, 64, 4096], P(('pair', 'blk')), may hold values from -6 to 6
- density: bfloat16 [12, 16384], P(None, 'blk'), may hold values from -0.75 to 0.75
- metric: bfloat16 [512, 512], P('pair'), may hold values from -0.5 to 0.5
- nu_local: int32 [32, 4, 2], P(('pair', 'blk')), may hold values from 0 to 63
- p_index: int32 [32, 4, 2], P(('pair', 'blk')), may hold values from 0 to 7
- counts: int32 [32, 4], P(('pair', 'blk')), may hold values from 0 to 2, as said below
Outputs:
- remapped: bfloat16 [8, 4, 512, 768], P(None, 'blk', 'pair')
The draws below stay inside these ranges and needn't reach their ends.
Inputs may be any that keep to these rules, and one draw needn't show every extreme that they name: `counts`: in every draw all panels of at least one orbital block are filled to 2.
All inputs are finite; a program needn't handle non-finite values.
Results may differ from the reference program's by a relative error of at most 0.0049.
Values may be sent and summed in bfloat16 or wider, within the bound.
A program may use at most 128 MiB of HBM per device.

```python
import jax
import jax.numpy as jnp
from jax import lax

BS = 64
NAO = 16384
SIG = 12
GCAP = 2
MUBS = 32
NUP = 64
PBLKS = 8
AUX = 512
N_PAIR = 8
N_BLK = 4


def draw_counts(key, part):
    key = jax.random.fold_in(key, 7)
    first_key, second_key = jax.random.split(key)
    base = jax.random.randint(first_key, (MUBS, N_BLK), 0, GCAP + 1, dtype=jnp.int32)
    chosen = jax.random.randint(second_key, (), 0, MUBS, dtype=jnp.int32)
    rows = jnp.arange(MUBS, dtype=jnp.int32)[:, None] == chosen
    return jnp.where(rows, GCAP, base).astype(jnp.int32)


def place_ends(values, key, least, largest):
    extent = values.shape
    spot = [jax.random.randint(jax.random.fold_in(key, axis), (), 0, extent[axis]) for axis in range(len(extent))]
    values = values.at[tuple(spot)].set(least)
    longest = extent.index(max(extent))
    spot[longest] = (spot[longest] + 1) % extent[longest]
    return values.at[tuple(spot)].set(largest)


def steps_of(key, dims, pieces, least, top_value):
    factor_of, own = 1.0, jax.random.fold_in(key, 6)
    for axis_at, blocks in pieces:
        heights = jnp.exp(jax.random.uniform(jax.random.fold_in(own, axis_at), (blocks,), jnp.float32, least / len(pieces), top_value / len(pieces)))
        factor_of = factor_of * jnp.repeat(heights, dims[axis_at] // blocks).reshape([-1 if axis == axis_at else 1 for axis in range(len(dims))])
    return factor_of


def normal_values(rng, shape, spread, bound, cuts=(), kind=jnp.bfloat16):
    gain = steps_of(rng, shape, cuts, -0.22, 0.18) if cuts else 1.0
    array = jax.random.normal(rng, shape, jnp.float32) * spread * gain
    return jnp.minimum(jnp.maximum(array, -bound), bound).astype(kind)


def setup_inputs(seed: int = 0) -> dict:
    key_of = jax.random.split(jax.random.key(seed), 7)
    integrals = normal_values(key_of[0], (MUBS, N_BLK, GCAP, BS, BS * BS), 1.0, 6.0, ((0, 32),))
    density = normal_values(key_of[1], (SIG, NAO), BS ** -0.5, 0.75, ((1, 4),))
    metric = normal_values(key_of[2], (AUX, AUX), (AUX // 4) ** -0.5, 0.5, ((0, 8),))
    nu_local = place_ends(jax.random.randint(key_of[3], (MUBS, N_BLK, GCAP), 0, NUP), jax.random.fold_in(key_of[3], 1), 0, NUP - 1).astype(jnp.int32)
    p_index = place_ends(jax.random.randint(key_of[4], (MUBS, N_BLK, GCAP), 0, PBLKS), jax.random.fold_in(key_of[4], 1), 0, PBLKS - 1).astype(jnp.int32)
    counts = draw_counts(jax.random.fold_in(key_of[6], 71), 0)
    return {"integrals": integrals, "density": density, "metric": metric, "nu_local": nu_local, "p_index": p_index, "counts": counts}


def reference(integrals, density, metric, nu_local, p_index, counts):
    offsets = jnp.arange(BS, dtype=jnp.int32)
    slot_ids = jnp.arange(GCAP, dtype=jnp.int32)

    def one_block(packed):
        block_data, nu_slots, aux_slots, filled = packed
        totals = jnp.zeros((PBLKS, BS * BS, SIG), jnp.float32)
        for group_id in range(N_BLK):
            first_cols = ((group_id * NUP + nu_slots[group_id]) * BS).astype(jnp.int32)
            col_index = first_cols[:, None] + offsets[None, :]
            dens_cols = jnp.take(density, col_index, axis=1).astype(jnp.float32)
            cube = block_data[group_id].astype(jnp.float32)
            contrib = jnp.einsum('sgn,gnx->gxs', dens_cols, cube)
            live_mask = (slot_ids < filled[group_id]).astype(jnp.float32)
            totals = totals.at[aux_slots[group_id]].add(contrib * live_mask[:, None, None])
        xmatrix = totals.astype(jnp.bfloat16).reshape(AUX, BS * SIG)
        product = lax.dot_general(metric, xmatrix, (((0,), (0,)), ((), ())), preferred_element_type=jnp.float32)
        return product.astype(jnp.bfloat16)

    results = lax.map(one_block, (integrals, nu_local, p_index, counts))
    return results.reshape(N_PAIR, N_BLK, AUX, SIG * BS)
```

```python
import functools

import jax
import jax.numpy as jnp
from jax import lax
from jax.experimental import pallas as pl
from jax.experimental.pallas import tpu as pltpu
from jax.sharding import PartitionSpec as P

MESH = pl.DeviceIdType.MESH
BF16 = jnp.bfloat16
F32 = jnp.float32


def offsets_far_first(count):
    return sorted(range(1, count), key=lambda off: -min(off, count - off))


def kernel(pairs, blks, nu_ref, p_ref, cnt_ref, ints_ref, dens_ref, metric_ref, out_ref,
           a_buf, dens_all, met_all, zbuf, xbuf, perm, ysend, lbuf,
           a_sem, dsend, drecv, msend, mrecv, ysems, yrecv, own_sem):
    q = lax.axis_index("pair")
    b = lax.axis_index("blk")
    core = lax.rem(b, 2)
    sib = b + 1 - 2 * core
    chips = blks // 2
    slots = p_ref.shape[2]
    bs = metric_ref.shape[0]
    half = bs // 2
    aux = metric_ref.shape[1]
    sig = dens_ref.shape[0]
    cols = sig * bs
    pn = aux // bs
    offs = offsets_far_first(pairs)
    slot_rows = slots * bs

    a_copies = []
    for g in range(blks):
        for k in range(slots):
            a_copies.append(pltpu.make_async_copy(
                ints_ref.at[0, g, k], a_buf.at[pl.ds((g * slots + k) * bs, bs), :], a_sem.at[g * slots + k]))
    for copy in a_copies:
        copy.start()

    barrier = pltpu.get_barrier_semaphore()
    for off in offs:
        pl.semaphore_signal(barrier, inc=1, device_id={"pair": lax.rem(q + off, pairs), "blk": b}, device_id_type=MESH)
    for j in range(1, chips):
        pl.semaphore_signal(barrier, inc=1, device_id={"pair": q, "blk": lax.rem(b + 2 * j, blks)}, device_id_type=MESH)
    pl.semaphore_signal(barrier, inc=1, device_id={"pair": q, "blk": sib}, device_id_type=MESH)

    t_id = lax.broadcasted_iota(jnp.int32, (half, bs), 0)
    i_id = lax.broadcasted_iota(jnp.int32, (half, bs), 1)
    pick = jnp.where(i_id == 2 * t_id + core, 1.0, 0.0).astype(BF16)
    mine = jnp.dot(pick, metric_ref[...], preferred_element_type=F32).astype(BF16)
    met_all[core, pl.ds(pl.multiple_of(q * half, half), half), :] = mine
    dens_all[b] = jnp.zeros(dens_all.shape[1:], BF16)
    dens_all[b, 0:sig, :] = dens_ref[...]

    pl.semaphore_wait(barrier, len(offs) + chips)

    d_out = []
    for j in range(chips):
        to = sib if j == 0 else lax.rem(b + 2 * j, blks)
        copy = pltpu.make_async_remote_copy(
            src_ref=dens_all.at[b], dst_ref=dens_all.at[b], send_sem=dsend.at[j], recv_sem=drecv.at[j],
            device_id={"pair": q, "blk": to}, device_id_type=MESH)
        copy.start()
        d_out.append(copy)
    m_out = []
    for n, off in enumerate(offs):
        part = met_all.at[core, pl.ds(pl.multiple_of(q * half, half), half), :]
        copy = pltpu.make_async_remote_copy(
            src_ref=part, dst_ref=part, send_sem=msend.at[n], recv_sem=mrecv.at[n],
            device_id={"pair": lax.rem(q + off, pairs), "blk": b}, device_id_type=MESH)
        copy.start()
        m_out.append(copy)

    lag = lax.broadcasted_iota(jnp.int32, (bs, cols), 1) - sig * lax.broadcasted_iota(jnp.int32, (bs, cols), 0)
    for s in range(sig):
        perm[s * bs:(s + 1) * bs, :] = jnp.where(lag == s, 1.0, 0.0).astype(BF16)

    for j in range(1, chips):
        src = lax.rem(b + blks - 2 * j, blks)
        pltpu.make_async_remote_copy(
            src_ref=dens_all.at[src], dst_ref=dens_all.at[src], send_sem=dsend.at[j], recv_sem=drecv.at[j],
            device_id={"pair": q, "blk": sib}, device_id_type=MESH).wait_recv()
        copy = pltpu.make_async_remote_copy(
            src_ref=dens_all.at[src], dst_ref=dens_all.at[src], send_sem=dsend.at[chips + j - 1],
            recv_sem=drecv.at[chips + j - 1], device_id={"pair": q, "blk": sib}, device_id_type=MESH)
        copy.start()
        d_out.append(copy)
    for j in range(chips):
        src = lax.rem(sib + blks - 2 * j, blks)
        pltpu.make_async_remote_copy(
            src_ref=dens_all.at[src], dst_ref=dens_all.at[src], send_sem=dsend.at[0],
            recv_sem=drecv.at[0 if j == 0 else chips + j - 1],
            device_id={"pair": q, "blk": sib}, device_id_type=MESH).wait_recv()

    lane = lax.broadcasted_iota(jnp.int32, (16, 128), 1)
    p_id = lax.broadcasted_iota(jnp.int32, (pn, 128), 0)
    p_lane = lax.broadcasted_iota(jnp.int32, (pn, 128), 1)
    for g in range(blks):
        filled = jnp.full((pn, 128), cnt_ref[0, g], jnp.int32)
        for k in range(0, slots, 2):
            nus = [jnp.full((16, 128), nu_ref[0, g, k + e], jnp.int32) for e in range(2)]
            found = [jnp.zeros((16, 128), F32), jnp.zeros((16, 128), F32)]
            for t in range(dens_ref.shape[1] // 128):
                tile = dens_all[g, :, t * 128:(t + 1) * 128].astype(F32)
                for e in range(2):
                    found[e] = jnp.where((nus[e] >> 1) == t, tile, found[e])
            tiles, marks = [], []
            for e in range(2):
                turned = pltpu.roll(found[e], 64, 1)
                tiles.append(jnp.where((nus[e] & 1) != e, turned, found[e]))
                target = jnp.full((pn, 128), p_ref[0, g, k + e], jnp.int32)
                marks.append(jnp.where(filled > k + e, target, -1))
            both = jnp.where(lane < 64, tiles[0], tiles[1])
            mask = jnp.where(p_lane < 64, marks[0], marks[1]) == p_id
            c0 = (g * slots + k) * bs
            for s in range(sig):
                row = jnp.broadcast_to(both[s:s + 1, :], (pn, 128))
                lbuf[s * pn:(s + 1) * pn, c0:c0 + 128] = jnp.where(mask, row, 0.0)

    for copy in a_copies:
        copy.wait()
    left = lbuf[...].astype(BF16)
    width = 512
    tiles_per = width // 128

    @pl.loop(0, bs * bs // width)
    def _(j):
        r = jnp.dot(left, a_buf[:, pl.ds(pl.multiple_of(j * width, width), width)], preferred_element_type=F32)
        for s in range(sig):
            for t in range(tiles_per):
                row0 = pl.multiple_of((s * half + j * tiles_per + t) * pn, 8)
                zbuf[pl.ds(row0, pn), :] = r[s * pn:(s + 1) * pn, t * 128:(t + 1) * 128]

    for n, off in enumerate(offs):
        src = lax.rem(q + pairs - off, pairs)
        part = met_all.at[core, pl.ds(pl.multiple_of(src * half, half), half), :]
        pltpu.make_async_remote_copy(
            src_ref=part, dst_ref=part, send_sem=msend.at[n], recv_sem=mrecv.at[n],
            device_id={"pair": q, "blk": sib}, device_id_type=MESH).wait_recv()
    last = len(offs)
    m_fwd = pltpu.make_async_remote_copy(
        src_ref=met_all.at[core], dst_ref=met_all.at[core], send_sem=msend.at[last], recv_sem=mrecv.at[last],
        device_id={"pair": q, "blk": sib}, device_id_type=MESH)
    m_fwd.start()
    m_out.append(m_fwd)

    low = lax.broadcasted_iota(jnp.int32, (half, 128), 1) < 64

    @pl.loop(0, pn)
    def _(p):
        for s in range(0, sig, 2):
            z0 = zbuf[pl.ds(s * half * pn + p, half, stride=pn), :]
            z1 = zbuf[pl.ds((s + 1) * half * pn + p, half, stride=pn), :]
            x0 = jnp.where(low, z0, pltpu.roll(z1, 64, 1))
            x1 = jnp.where(low, pltpu.roll(z0, 64, 1), z1)
            at = pl.ds(pl.multiple_of(p * half, half), half)
            xbuf[0, at, s * bs:s * bs + 128] = x0.astype(BF16)
            xbuf[1, at, s * bs:s * bs + 128] = x1.astype(BF16)

    pltpu.make_async_remote_copy(
        src_ref=met_all.at[1 - core], dst_ref=met_all.at[1 - core], send_sem=msend.at[last], recv_sem=mrecv.at[last],
        device_id={"pair": q, "blk": sib}, device_id_type=MESH).wait_recv()

    block = 256
    parts = cols // block
    y_out = []
    for c in range(parts):
        span = slice(c * block, (c + 1) * block)
        total = None
        for h in range(2):
            xp = jnp.dot(xbuf[h], perm[:, span], preferred_element_type=F32).astype(BF16)
            term = lax.dot_general(met_all[h], xp, (((0,), (0,)), ((), ())), preferred_element_type=F32)
            total = term if total is None else total + term
        ysend[c] = total.astype(BF16).reshape(pairs, bs, block)
        for n, off in enumerate(offs):
            to = lax.rem(q + off, pairs)
            copy = pltpu.make_async_remote_copy(
                src_ref=ysend.at[c, to], dst_ref=out_ref.at[q, 0, :, span], send_sem=ysems.at[c, n],
                recv_sem=yrecv.at[c, n], device_id={"pair": to, "blk": b}, device_id_type=MESH)
            copy.start()
            y_out.append(copy)
        copy = pltpu.make_async_copy(ysend.at[c, q], out_ref.at[q, 0, :, span], own_sem.at[c])
        copy.start()

    for c in range(parts):
        span = slice(c * block, (c + 1) * block)
        for n, off in enumerate(offs):
            src = lax.rem(q + pairs - off, pairs)
            pltpu.make_async_remote_copy(
                src_ref=ysend.at[c, src], dst_ref=out_ref.at[src, 0, :, span], send_sem=ysems.at[c, n],
                recv_sem=yrecv.at[c, n], device_id={"pair": src, "blk": b}, device_id_type=MESH).wait_recv()
        pltpu.make_async_copy(ysend.at[c, q], out_ref.at[q, 0, :, span], own_sem.at[c]).wait()
    for copy in d_out + m_out + y_out:
        copy.wait_send()


def solution(mesh):
    pairs, blks = mesh.shape["pair"], mesh.shape["blk"]

    def per_device(integrals, density, metric, nu_local, p_index, counts):
        _, groups, slots, bs, wide = integrals.shape
        sig, panel = density.shape
        aux = metric.shape[1]
        cols = sig * bs
        pn = aux // bs
        half = bs // 2
        n_off = pairs - 1
        chips = blks // 2
        block = 256
        parts = cols // block
        vmem = pl.BlockSpec(memory_space=pltpu.VMEM)
        smem = pl.BlockSpec(memory_space=pltpu.SMEM)
        anyw = pl.BlockSpec(memory_space=pl.ANY)
        dma = pltpu.SemaphoreType.DMA
        return pl.pallas_call(
            functools.partial(kernel, pairs, blks),
            out_shape=jax.ShapeDtypeStruct((pairs, 1, bs, cols), BF16),
            in_specs=[smem, smem, smem, anyw, vmem, vmem],
            out_specs=anyw,
            scratch_shapes=[
                pltpu.VMEM((groups * slots * bs, wide), BF16),
                pltpu.VMEM((blks, 16, panel), BF16),
                pltpu.VMEM((2, pn * half, aux), BF16),
                pltpu.VMEM((sig * half * pn, 128), F32),
                pltpu.VMEM((2, pn * half, cols), BF16),
                pltpu.VMEM((cols, cols), BF16),
                pltpu.VMEM((parts, pairs, bs, block), BF16),
                pltpu.VMEM((sig * pn, groups * slots * bs), F32),
                dma((groups * slots,)),
                dma((2 * chips,)),
                dma((2 * chips,)),
                dma((n_off + 1,)),
                dma((n_off + 1,)),
                dma((parts, n_off)),
                dma((parts, n_off)),
                dma((parts,)),
            ],
            compiler_params=pltpu.CompilerParams(
                collective_id=0, has_side_effects=True, vmem_limit_bytes=56 * 1024 * 1024
            ),
            cost_estimate=pl.CostEstimate(flops=2000000000, bytes_accessed=6000000, transcendentals=0),
        )(nu_local, p_index, counts, integrals, density, metric)

    in_specs = (
        P(("pair", "blk"), None, None, None, None),
        P(None, "blk"),
        P("pair", None),
        P(("pair", "blk"), None, None),
        P(("pair", "blk"), None, None),
        P(("pair", "blk"), None),
    )
    return jax.shard_map(
        per_device, mesh=mesh, in_specs=in_specs, out_specs=P(None, "blk", "pair", None), check_vma=False
    )
```

```python
import functools

import jax
import jax.numpy as jnp
from jax import lax
from jax.experimental import pallas as pl
from jax.experimental.pallas import tpu as pltpu
from jax.sharding import PartitionSpec as P

MESH = pl.DeviceIdType.MESH
BF16 = jnp.bfloat16
F32 = jnp.float32


def offsets_far_first(count):
    return sorted(range(1, count), key=lambda off: -min(off, count - off))


def kernel(pairs, blks, nu_ref, p_ref, cnt_ref, ints_ref, dens_ref, metric_ref, out_ref,
           a_buf, dens_pad, req_out, req_in, rep_out, rep_in, met_all, met_t, zbuf, xbuf, perm, ysend, lbuf,
           a_sem, req_s, req_r, rep_s, rep_r, msend, mrecv, fsend, frecv, ysems, yrecv, own_sem):
    q = lax.axis_index("pair")
    b = lax.axis_index("blk")
    core = lax.rem(b, 2)
    sib = b + 1 - 2 * core
    slots = p_ref.shape[1]
    bs = metric_ref.shape[0]
    half = bs // 2
    aux = metric_ref.shape[1]
    sig = dens_ref.shape[0]
    cols = sig * bs
    pn = aux // bs
    offs = offsets_far_first(pairs)

    a_copies = []
    for g in range(blks):
        for k in range(slots):
            a_copies.append(pltpu.make_async_copy(
                ints_ref.at[0, g, k], a_buf.at[pl.ds((g * slots + k) * bs, bs), :], a_sem.at[g * slots + k]))
    for copy in a_copies:
        copy.start()

    barrier = pltpu.get_barrier_semaphore()
    for off in offs:
        pl.semaphore_signal(barrier, inc=1, device_id={"pair": lax.rem(q + off, pairs), "blk": b}, device_id_type=MESH)
    for j in range(1, blks):
        pl.semaphore_signal(barrier, inc=1, device_id={"pair": q, "blk": lax.rem(b + j, blks)}, device_id_type=MESH)

    row_id = lax.broadcasted_iota(jnp.int32, (8, 128), 0)
    for j in range(1, blks):
        g = lax.rem(b + j, blks)
        tile = jnp.full((8, 128), nu_ref[0, 0, g], jnp.int32)
        for k in range(1, slots):
            tile = jnp.where(row_id == k, nu_ref[0, k, g], tile)
        req_out[j] = tile

    t_id = lax.broadcasted_iota(jnp.int32, (half, bs), 0)
    i_id = lax.broadcasted_iota(jnp.int32, (half, bs), 1)
    pick = jnp.where(i_id == 2 * t_id + core, 1.0, 0.0).astype(BF16)
    mine = jnp.dot(pick, metric_ref[...], preferred_element_type=F32).astype(BF16)
    met_all[core, pl.ds(pl.multiple_of(q * half, half), half), :] = mine
    dens_pad[...] = jnp.zeros(dens_pad.shape, BF16)
    dens_pad[0:sig, :] = dens_ref[...]

    pl.semaphore_wait(barrier, len(offs) + blks - 1)

    def blk_copy(src, dst, send, recv, j, to):
        return pltpu.make_async_remote_copy(
            src_ref=src.at[j], dst_ref=dst.at[j], send_sem=send.at[j], recv_sem=recv.at[j],
            device_id={"pair": q, "blk": to}, device_id_type=MESH)

    sent = []
    for j in range(1, blks):
        copy = blk_copy(req_out, req_in, req_s, req_r, j, lax.rem(b + j, blks))
        copy.start()
        sent.append(copy)
    m_out = []
    for n, off in enumerate(offs):
        part = met_all.at[core, pl.ds(pl.multiple_of(q * half, half), half), :]
        copy = pltpu.make_async_remote_copy(
            src_ref=part, dst_ref=part, send_sem=msend.at[n], recv_sem=mrecv.at[n],
            device_id={"pair": lax.rem(q + off, pairs), "blk": b}, device_id_type=MESH)
        copy.start()
        m_out.append(copy)

    def to_sibling(half_id, src, n):
        part = met_all.at[half_id, pl.ds(pl.multiple_of(src * half, half), half), :]
        return pltpu.make_async_remote_copy(
            src_ref=part, dst_ref=part, send_sem=fsend.at[n], recv_sem=frecv.at[n],
            device_id={"pair": q, "blk": sib}, device_id_type=MESH)

    copy = to_sibling(core, q, len(offs))
    copy.start()
    m_out.append(copy)

    lane = lax.broadcasted_iota(jnp.int32, (16, 128), 1)

    def columns_of(indices):
        found = [[jnp.zeros((16, 128), F32) for _ in range(slots)] for _ in indices]
        for t in range(dens_ref.shape[1] // 128):
            tile = dens_pad[:, t * 128:(t + 1) * 128].astype(F32)
            for a, nus in enumerate(indices):
                for k in range(slots):
                    found[a][k] = jnp.where((nus[k] >> 1) == t, tile, found[a][k])
        out = []
        for a, nus in enumerate(indices):
            sides = []
            for k in range(slots):
                turned = pltpu.roll(found[a][k], 64, 1)
                sides.append(jnp.where((nus[k] & 1) != k, turned, found[a][k]))
            out.append(jnp.where(lane < 64, sides[0], sides[1]))
        return out

    p_id = lax.broadcasted_iota(jnp.int32, (pn, 128), 0)
    p_lane = lax.broadcasted_iota(jnp.int32, (pn, 128), 1)

    def put(g, both):
        filled = jnp.full((pn, 128), cnt_ref[0, g], jnp.int32)
        marks = [jnp.where(filled > k, jnp.full((pn, 128), p_ref[0, k, g], jnp.int32), -1) for k in range(slots)]
        mask = jnp.where(p_lane < 64, marks[0], marks[1]) == p_id
        at = pl.ds(pl.multiple_of(g * 128, 128), 128)
        for s in range(sig):
            row = jnp.broadcast_to(both[s:s + 1, :], (pn, 128))
            lbuf[s * pn:(s + 1) * pn, at] = jnp.where(mask, row, 0.0)

    own = columns_of([[jnp.full((16, 128), nu_ref[0, k, b], jnp.int32) for k in range(slots)]])
    put(b, own[0])
    for j in range(1, blks):
        blk_copy(req_out, req_in, req_s, req_r, j, lax.rem(b + j, blks)).wait_recv()
    asked = [[jnp.broadcast_to(req_in[j, k:k + 1, :], (16, 128)) for k in range(slots)] for j in range(1, blks)]
    for first in range(0, blks - 1, 4):
        for n, both in enumerate(columns_of(asked[first:first + 4])):
            j = first + n + 1
            rep_out[j] = both.astype(BF16)
            copy = blk_copy(rep_out, rep_in, rep_s, rep_r, j, lax.rem(b + blks - j, blks))
            copy.start()
            sent.append(copy)

    lag = lax.broadcasted_iota(jnp.int32, (bs, cols), 1) - sig * lax.broadcasted_iota(jnp.int32, (bs, cols), 0)
    for s in range(sig):
        perm[s * bs:(s + 1) * bs, :] = jnp.where(lag == s, 1.0, 0.0).astype(BF16)

    for j in range(1, blks):
        blk_copy(rep_out, rep_in, rep_s, rep_r, j, lax.rem(b + j, blks)).wait_recv()
        put(lax.rem(b + j, blks), rep_in[j].astype(F32))

    for copy in a_copies:
        copy.wait()
    left = lbuf[...].astype(BF16)
    width = 512
    tiles_per = width // 128

    @pl.loop(0, bs * bs // width)
    def _(j):
        r = jnp.dot(left, a_buf[:, pl.ds(pl.multiple_of(j * width, width), width)], preferred_element_type=F32)
        for s in range(sig):
            for t in range(tiles_per):
                row0 = pl.multiple_of((s * half + j * tiles_per + t) * pn, 8)
                zbuf[pl.ds(row0, pn), :] = r[s * pn:(s + 1) * pn, t * 128:(t + 1) * 128]

    for n, off in enumerate(offs):
        src = lax.rem(q + pairs - off, pairs)
        part = met_all.at[core, pl.ds(pl.multiple_of(src * half, half), half), :]
        pltpu.make_async_remote_copy(
            src_ref=part, dst_ref=part, send_sem=msend.at[n], recv_sem=mrecv.at[n],
            device_id={"pair": q, "blk": sib}, device_id_type=MESH).wait_recv()
        copy = to_sibling(core, src, n)
        copy.start()
        m_out.append(copy)

    low = lax.broadcasted_iota(jnp.int32, (half, 128), 1) < 64

    @pl.loop(0, pn)
    def _(p):
        for s in range(0, sig, 2):
            z0 = zbuf[pl.ds(s * half * pn + p, half, stride=pn), :]
            z1 = zbuf[pl.ds((s + 1) * half * pn + p, half, stride=pn), :]
            x0 = jnp.where(low, z0, pltpu.roll(z1, 64, 1))
            x1 = jnp.where(low, pltpu.roll(z0, 64, 1), z1)
            at = pl.ds(pl.multiple_of(p * half, half), half)
            xbuf[0, at, s * bs:s * bs + 128] = x0.astype(BF16)
            xbuf[1, at, s * bs:s * bs + 128] = x1.astype(BF16)

    met_t[core] = met_all[core].T
    for n, off in enumerate(offs + [0]):
        to_sibling(1 - core, lax.rem(q + pairs - off, pairs), n).wait_recv()
    met_t[1 - core] = met_all[1 - core].T

    block = 256
    parts = cols // block
    y_out = []
    for c in range(parts):
        span = slice(c * block, (c + 1) * block)
        total = None
        for h in range(2):
            xp = jnp.dot(xbuf[h], perm[:, span], preferred_element_type=F32).astype(BF16)
            term = jnp.dot(met_t[h], xp, preferred_element_type=F32)
            total = term if total is None else total + term
        ysend[c] = total.astype(BF16).reshape(pairs, bs, block)
        for n, off in enumerate(offs):
            to = lax.rem(q + off, pairs)
            copy = pltpu.make_async_remote_copy(
                src_ref=ysend.at[c, to], dst_ref=out_ref.at[q, 0, :, span], send_sem=ysems.at[c, n],
                recv_sem=yrecv.at[c, n], device_id={"pair": to, "blk": b}, device_id_type=MESH)
            copy.start()
            y_out.append(copy)
        copy = pltpu.make_async_copy(ysend.at[c, q], out_ref.at[q, 0, :, span], own_sem.at[c])
        copy.start()

    for c in range(parts):
        span = slice(c * block, (c + 1) * block)
        for n, off in enumerate(offs):
            src = lax.rem(q + pairs - off, pairs)
            pltpu.make_async_remote_copy(
                src_ref=ysend.at[c, src], dst_ref=out_ref.at[src, 0, :, span], send_sem=ysems.at[c, n],
                recv_sem=yrecv.at[c, n], device_id={"pair": src, "blk": b}, device_id_type=MESH).wait_recv()
        pltpu.make_async_copy(ysend.at[c, q], out_ref.at[q, 0, :, span], own_sem.at[c]).wait()
    for copy in sent + m_out + y_out:
        copy.wait_send()


def solution(mesh):
    pairs, blks = mesh.shape["pair"], mesh.shape["blk"]

    def per_device(integrals, density, metric, nu_local, p_index, counts):
        _, groups, slots, bs, wide = integrals.shape
        sig, panel = density.shape
        aux = metric.shape[1]
        cols = sig * bs
        pn = aux // bs
        half = bs // 2
        n_off = pairs - 1
        block = 256
        parts = cols // block
        vmem = pl.BlockSpec(memory_space=pltpu.VMEM)
        smem = pl.BlockSpec(memory_space=pltpu.SMEM)
        anyw = pl.BlockSpec(memory_space=pl.ANY)
        dma = pltpu.SemaphoreType.DMA
        return pl.pallas_call(
            functools.partial(kernel, pairs, blks),
            out_shape=pltpu.VMEM((pairs, 1, bs, cols), BF16),
            in_specs=[smem, smem, smem, anyw, vmem, vmem],
            out_specs=vmem,
            scratch_shapes=[
                pltpu.VMEM((groups * slots * bs, wide), BF16),
                pltpu.VMEM((16, panel), BF16),
                pltpu.VMEM((blks, 8, 128), jnp.int32),
                pltpu.VMEM((blks, 8, 128), jnp.int32),
                pltpu.VMEM((blks, 16, 128), BF16),
                pltpu.VMEM((blks, 16, 128), BF16),
                pltpu.VMEM((2, pn * half, aux), BF16),
                pltpu.VMEM((2, aux, pn * half), BF16),
                pltpu.VMEM((sig * half * pn, 128), F32),
                pltpu.VMEM((2, pn * half, cols), BF16),
                pltpu.VMEM((cols, cols), BF16),
                pltpu.VMEM((parts, pairs, bs, block), BF16),
                pltpu.VMEM((sig * pn, groups * slots * bs), F32),
                dma((groups * slots,)),
                dma((blks,)),
                dma((blks,)),
                dma((blks,)),
                dma((blks,)),
                dma((n_off,)),
                dma((n_off,)),
                dma((n_off + 1,)),
                dma((n_off + 1,)),
                dma((parts, n_off)),
                dma((parts, n_off)),
                dma((parts,)),
            ],
            compiler_params=pltpu.CompilerParams(
                collective_id=0, has_side_effects=True, vmem_limit_bytes=56 * 1024 * 1024
            ),
            cost_estimate=pl.CostEstimate(flops=2000000000, bytes_accessed=6000000, transcendentals=0),
        )(jnp.swapaxes(nu_local, 1, 2), jnp.swapaxes(p_index, 1, 2), counts, integrals, density, metric)

    in_specs = (
        P(("pair", "blk"), None, None, None, None),
        P(None, "blk"),
        P("pair", None),
        P(("pair", "blk"), None, None),
        P(("pair", "blk"), None, None),
        P(("pair", "blk"), None),
    )
    return jax.shard_map(
        per_device, mesh=mesh, in_specs=in_specs, out_specs=P(None, "blk", "pair", None), check_vma=False
    )
```

```python
import functools

import jax
import jax.numpy as jnp
from jax import lax
from jax.experimental import pallas as pl
from jax.experimental.pallas import tpu as pltpu
from jax.sharding import PartitionSpec as P

MESH = pl.DeviceIdType.MESH
BF16 = jnp.bfloat16
F32 = jnp.float32


def offsets_far_first(count):
    return sorted(range(1, count), key=lambda off: -min(off, count - off))


def kernel(pairs, blks, nu_ref, p_ref, cnt_ref, ints_ref, dens_ref, metric_ref, out_ref,
           a_buf, dens_in, met_in, req_out, req_in, rep_out, rep_in, met_all, met_t, order, xbuf, perm, ysend, lbuf,
           a_sem, in_sem, req_s, req_r, rep_s, rep_r, msend, mrecv, fsend, frecv, ysems, yrecv, own_sem):
    q = lax.axis_index("pair")
    b = lax.axis_index("blk")
    core = lax.rem(b, 2)
    sib = b + 1 - 2 * core
    slots = p_ref.shape[1]
    bs = metric_ref.shape[0]
    half = bs // 2
    aux = metric_ref.shape[1]
    sig = dens_ref.shape[0]
    cols = sig * bs
    pn = aux // bs
    offs = offsets_far_first(pairs)

    a_copies = []
    for g in range(blks):
        for k in range(slots):
            a_copies.append(pltpu.make_async_copy(
                ints_ref.at[0, g, k], a_buf.at[pl.ds((g * slots + k) * bs, bs), :], a_sem.at[g * slots + k]))

    barrier = pltpu.get_barrier_semaphore()
    for off in offs:
        pl.semaphore_signal(barrier, inc=1, device_id={"pair": lax.rem(q + off, pairs), "blk": b}, device_id_type=MESH)
    for j in range(1, blks):
        pl.semaphore_signal(barrier, inc=1, device_id={"pair": q, "blk": lax.rem(b + j, blks)}, device_id_type=MESH)

    dens_load = pltpu.make_async_copy(dens_ref, dens_in, in_sem.at[0])
    met_load = pltpu.make_async_copy(metric_ref, met_in, in_sem.at[1])
    met_load.start()
    dens_load.start()
    for copy in a_copies:
        copy.start()

    row_id = lax.broadcasted_iota(jnp.int32, (8, 128), 0)
    for j in range(1, blks):
        g = lax.rem(b + j, blks)
        tile = jnp.full((8, 128), nu_ref[0, 0, g], jnp.int32)
        for k in range(1, slots):
            tile = jnp.where(row_id == k, nu_ref[0, k, g], tile)
        req_out[j] = tile

    pl.semaphore_wait(barrier, len(offs) + blks - 1)

    def blk_copy(src, dst, send, recv, j, to):
        return pltpu.make_async_remote_copy(
            src_ref=src.at[j], dst_ref=dst.at[j], send_sem=send.at[j], recv_sem=recv.at[j],
            device_id={"pair": q, "blk": to}, device_id_type=MESH)

    rep_out[...] = jnp.zeros(rep_out.shape, BF16)
    sent = []
    for j in range(1, blks):
        copy = blk_copy(req_out, req_in, req_s, req_r, j, lax.rem(b + j, blks))
        copy.start()
        sent.append(copy)
    t_id = lax.broadcasted_iota(jnp.int32, (half, bs), 0)
    i_id = lax.broadcasted_iota(jnp.int32, (half, bs), 1)
    pick = jnp.where(i_id == 2 * t_id + core, 1.0, 0.0).astype(BF16)
    met_load.wait()
    mine = jnp.dot(pick, met_in[...], preferred_element_type=F32).astype(BF16)
    met_all[core, pl.ds(pl.multiple_of(q * half, half), half), :] = mine
    m_out = []
    for n, off in enumerate(offs):
        part = met_all.at[core, pl.ds(pl.multiple_of(q * half, half), half), :]
        copy = pltpu.make_async_remote_copy(
            src_ref=part, dst_ref=part, send_sem=msend.at[n], recv_sem=mrecv.at[n],
            device_id={"pair": lax.rem(q + off, pairs), "blk": b}, device_id_type=MESH)
        copy.start()
        m_out.append(copy)

    def to_sibling(half_id, src, n):
        part = met_all.at[half_id, pl.ds(pl.multiple_of(src * half, half), half), :]
        return pltpu.make_async_remote_copy(
            src_ref=part, dst_ref=part, send_sem=fsend.at[n], recv_sem=frecv.at[n],
            device_id={"pair": q, "blk": sib}, device_id_type=MESH)


    lane = lax.broadcasted_iota(jnp.int32, (sig, 128), 1)
    dens_load.wait()

    def columns_of(indices):
        found = [[jnp.zeros((sig, 128), F32) for _ in range(slots)] for _ in indices]
        for t in range(dens_ref.shape[1] // 128):
            tile = dens_in[:, t * 128:(t + 1) * 128].astype(F32)
            for a, nus in enumerate(indices):
                for k in range(slots):
                    found[a][k] = jnp.where((nus[k] >> 1) == t, tile, found[a][k])
        out = []
        for a, nus in enumerate(indices):
            sides = []
            for k in range(slots):
                turned = pltpu.roll(found[a][k], 64, 1)
                sides.append(jnp.where((nus[k] & 1) != k, turned, found[a][k]))
            out.append(jnp.where(lane < 64, sides[0], sides[1]))
        return out

    p_id = lax.broadcasted_iota(jnp.int32, (pn, 128), 0)
    p_lane = lax.broadcasted_iota(jnp.int32, (pn, 128), 1)

    def put(g, both):
        filled = jnp.full((pn, 128), cnt_ref[0, g], jnp.int32)
        marks = [jnp.where(filled > k, jnp.full((pn, 128), p_ref[0, k, g], jnp.int32), -1) for k in range(slots)]
        mask = jnp.where(p_lane < 64, marks[0], marks[1]) == p_id
        at = pl.ds(pl.multiple_of(g * 128, 128), 128)
        for s in range(sig):
            row = jnp.broadcast_to(both[s:s + 1, :], (pn, 128))
            lbuf[s * pn:(s + 1) * pn, at] = jnp.where(mask, row, 0.0)

    own = columns_of([[jnp.full((sig, 128), nu_ref[0, k, b], jnp.int32) for k in range(slots)]])
    put(b, own[0])
    for j in range(1, blks):
        blk_copy(req_out, req_in, req_s, req_r, j, lax.rem(b + j, blks)).wait_recv()
    asked = [[jnp.broadcast_to(req_in[j, k:k + 1, :], (sig, 128)) for k in range(slots)] for j in range(1, blks)]
    for first in range(0, blks - 1, 4):
        for n, both in enumerate(columns_of(asked[first:first + 4])):
            j = first + n + 1
            rep_out[j, 0:sig, :] = both.astype(BF16)
            copy = blk_copy(rep_out, rep_in, rep_s, rep_r, j, lax.rem(b + blks - j, blks))
            copy.start()
            sent.append(copy)

    lag = lax.broadcasted_iota(jnp.int32, (bs, cols), 1) - sig * lax.broadcasted_iota(jnp.int32, (bs, cols), 0)
    for s in range(sig):
        perm[s * bs:(s + 1) * bs, :] = jnp.where(lag == s, 1.0, 0.0).astype(BF16)

    shift = pn.bit_length() - 1
    r_id = lax.broadcasted_iota(jnp.int32, order.shape, 0)
    c_id = lax.broadcasted_iota(jnp.int32, order.shape, 1)
    order[...] = jnp.where(c_id == (r_id & (pn - 1)) * half + (r_id >> shift), 1.0, 0.0).astype(BF16)

    for j in range(1, blks):
        blk_copy(rep_out, rep_in, rep_s, rep_r, j, lax.rem(b + j, blks)).wait_recv()
        put(lax.rem(b + j, blks), rep_in[j].astype(F32))

    for copy in a_copies:
        copy.wait()
    left = lbuf[...].astype(BF16)
    width = 512
    tiles_per = width // 128
    low = lax.broadcasted_iota(jnp.int32, (tiles_per * pn, 128), 1) < 64

    @pl.loop(0, bs * bs // width)
    def _(j):
        r = jnp.dot(left, a_buf[:, pl.ds(pl.multiple_of(j * width, width), width)], preferred_element_type=F32)
        at = pl.ds(pl.multiple_of(j * tiles_per * pn, tiles_per * pn), tiles_per * pn)
        for s in range(0, sig, 2):
            z0, z1 = [jnp.concatenate(
                [r[e * pn:(e + 1) * pn, t * 128:(t + 1) * 128] for t in range(tiles_per)], 0) for e in (s, s + 1)]
            x0 = jnp.where(low, z0, pltpu.roll(z1, 64, 1))
            x1 = jnp.where(low, pltpu.roll(z0, 64, 1), z1)
            xbuf[0, at, s * bs:s * bs + 128] = x0.astype(BF16)
            xbuf[1, at, s * bs:s * bs + 128] = x1.astype(BF16)

    for n, off in enumerate(offs):
        src = lax.rem(q + pairs - off, pairs)
        part = met_all.at[core, pl.ds(pl.multiple_of(src * half, half), half), :]
        pltpu.make_async_remote_copy(
            src_ref=part, dst_ref=part, send_sem=msend.at[n], recv_sem=mrecv.at[n],
            device_id={"pair": q, "blk": sib}, device_id_type=MESH).wait_recv()

    whole_half = [pltpu.make_async_remote_copy(
        src_ref=met_all.at[h], dst_ref=met_all.at[h], send_sem=fsend.at[0], recv_sem=frecv.at[0],
        device_id={"pair": q, "blk": sib}, device_id_type=MESH) for h in (core, 1 - core)]
    whole_half[0].start()
    m_out.append(whole_half[0])
    xfirst = [jnp.dot(xbuf[h], perm[:, 0:768], preferred_element_type=F32).astype(BF16) for h in range(2)]
    met_t[core] = jnp.dot(order[...], met_all[core], preferred_element_type=F32).astype(BF16).T
    whole_half[1].wait_recv()
    met_t[1 - core] = jnp.dot(order[...], met_all[1 - core], preferred_element_type=F32).astype(BF16).T

    block = 768
    parts = cols // block
    y_out = []
    for c in range(parts):
        span = slice(c * block, (c + 1) * block)
        total = None
        for h in range(2):
            if c == 0:
                xp = xfirst[h]
            else:
                xp = jnp.dot(xbuf[h], perm[:, span], preferred_element_type=F32).astype(BF16)
            term = jnp.dot(met_t[h], xp, preferred_element_type=F32)
            total = term if total is None else total + term
        ysend[c] = total.astype(BF16).reshape(pairs, bs, block)
        for n, off in enumerate(offs):
            to = lax.rem(q + off, pairs)
            copy = pltpu.make_async_remote_copy(
                src_ref=ysend.at[c, to], dst_ref=out_ref.at[q, 0, :, span], send_sem=ysems.at[c, n],
                recv_sem=yrecv.at[c, n], device_id={"pair": to, "blk": b}, device_id_type=MESH)
            copy.start()
            y_out.append(copy)
        copy = pltpu.make_async_copy(ysend.at[c, q], out_ref.at[q, 0, :, span], own_sem.at[c])
        copy.start()

    for c in range(parts):
        span = slice(c * block, (c + 1) * block)
        for n, off in enumerate(offs):
            src = lax.rem(q + pairs - off, pairs)
            pltpu.make_async_remote_copy(
                src_ref=ysend.at[c, src], dst_ref=out_ref.at[src, 0, :, span], send_sem=ysems.at[c, n],
                recv_sem=yrecv.at[c, n], device_id={"pair": src, "blk": b}, device_id_type=MESH).wait_recv()
        pltpu.make_async_copy(ysend.at[c, q], out_ref.at[q, 0, :, span], own_sem.at[c]).wait()
    for copy in sent + m_out + y_out:
        copy.wait_send()


def solution(mesh):
    pairs, blks = mesh.shape["pair"], mesh.shape["blk"]

    def per_device(integrals, density, metric, nu_local, p_index, counts):
        _, groups, slots, bs, wide = integrals.shape
        sig, panel = density.shape
        aux = metric.shape[1]
        cols = sig * bs
        pn = aux // bs
        half = bs // 2
        n_off = pairs - 1
        block = 768
        parts = cols // block
        vmem = pl.BlockSpec(memory_space=pltpu.VMEM)
        smem = pl.BlockSpec(memory_space=pltpu.SMEM)
        anyw = pl.BlockSpec(memory_space=pl.ANY)
        dma = pltpu.SemaphoreType.DMA
        return pl.pallas_call(
            functools.partial(kernel, pairs, blks),
            out_shape=pltpu.VMEM((pairs, 1, bs, cols), BF16),
            in_specs=[smem, smem, smem, anyw, anyw, anyw],
            out_specs=vmem,
            scratch_shapes=[
                pltpu.VMEM((groups * slots * bs, wide), BF16),
                pltpu.VMEM((sig, panel), BF16),
                pltpu.VMEM((bs, aux), BF16),
                pltpu.VMEM((blks, 8, 128), jnp.int32),
                pltpu.VMEM((blks, 8, 128), jnp.int32),
                pltpu.VMEM((blks, 16, 128), BF16),
                pltpu.VMEM((blks, 16, 128), BF16),
                pltpu.VMEM((2, pn * half, aux), BF16),
                pltpu.VMEM((2, aux, pn * half), BF16),
                pltpu.VMEM((pn * half, pn * half), BF16),
                pltpu.VMEM((2, pn * half, cols), BF16),
                pltpu.VMEM((cols, cols), BF16),
                pltpu.VMEM((parts, pairs, bs, block), BF16),
                pltpu.VMEM((sig * pn, groups * slots * bs), F32),
                dma((groups * slots,)),
                dma((2,)),
                dma((blks,)),
                dma((blks,)),
                dma((blks,)),
                dma((blks,)),
                dma((n_off,)),
                dma((n_off,)),
                dma((1,)),
                dma((1,)),
                dma((parts, n_off)),
                dma((parts, n_off)),
                dma((parts,)),
            ],
            compiler_params=pltpu.CompilerParams(
                collective_id=0, has_side_effects=True, vmem_limit_bytes=56 * 1024 * 1024
            ),
            cost_estimate=pl.CostEstimate(flops=2000000000, bytes_accessed=6000000, transcendentals=0),
        )(jnp.swapaxes(nu_local, 1, 2), jnp.swapaxes(p_index, 1, 2), counts, integrals, density, metric)

    in_specs = (
        P(("pair", "blk"), None, None, None, None),
        P(None, "blk"),
        P("pair", None),
        P(("pair", "blk"), None, None),
        P(("pair", "blk"), None, None),
        P(("pair", "blk"), None),
    )
    return jax.shard_map(
        per_device, mesh=mesh, in_specs=in_specs, out_specs=P(None, "blk", "pair", None), check_vma=False
    )
```
